256 devices in a mesh: blk: 64 (over z, x, y_hi), inner: 4 (over y_lo, core).
Axes of the slice: x: 4, y: 4 (y_hi: 2, y_lo: 2; y = y_hi * 2 + y_lo), z: 8, core: 2. Of those that a mesh axis runs over, the one named last changes fastest.
Arguments:
- image_embeds: bfloat16 [81920, 1152], P(('blk', 'inner')), may hold values from -0.59765625 to 0.59765625
- text_embeds: bfloat16 [81920, 1152], P(('blk', 'inner')), may hold values from -0.59765625 to 0.59765625
- positive: int32 [81920], P(('blk', 'inner')), may hold values from 0 to 1279, as said below
- logit_scale: float32 [1], replicated, may hold values from 2 to 4
- logit_bias: float32 [1], replicated, may hold values from -2 to -0.5
Outputs:
- grad_images: float32 [81920, 1152], P(('blk', 'inner'))
- grad_texts: float32 [81920, 1152], P(('blk', 'inner'))
The draws below stay inside these ranges and needn't reach their ends.
Inputs may be any that keep to these rules, and one draw needn't show every extreme that they name: `positive`: within each aligned block of 1280 entries every value 0 .. 1279 appears exactly once.
All inputs are finite; a program needn't handle non-finite values.
Results may differ from the reference program's by a relative error of at most 0.0024.
Values may be sent and summed in bfloat16 or wider, within the bound.
No kernel may reach another device: no remote copies, remote signals or barrier semaphores. Data moves between devices by JAX's collectives and lax.ppermute only.
A program may use at most 64 MiB of HBM per device.

```python
import jax
import jax.numpy as jnp
from jax import lax

D = 1152
STEPS = 3
GROUP = 1280
TOKENS = 81920


def draw_positive(key, part):
    key = jax.random.fold_in(key, 7)
    keys = jax.random.split(key, TOKENS // GROUP)
    orders = jax.vmap(lambda one_key: jax.random.permutation(one_key, GROUP))(keys)
    return orders.astype(jnp.int32).reshape(TOKENS)


def levels(rng, shape, cuts, smallest, top_value):
    gain, own = 1.0, jax.random.fold_in(rng, 6)
    for axis_at, parts in cuts:
        draws = jnp.exp(jax.random.uniform(jax.random.fold_in(own, axis_at), (parts,), jnp.float32, smallest / len(cuts), top_value / len(cuts)))
        gain = gain * jnp.repeat(draws, shape[axis_at] // parts).reshape([-1 if axis == axis_at else 1 for axis in range(len(shape))])
    return gain


def noise(key, shape, scale, bound, cuts=(), kind=jnp.bfloat16):
    result = jax.random.normal(key, shape, jnp.float32) * scale
    if len(cuts) > 0:
        result = levels(key, shape, cuts, -0.22, 0.18) * result
    return jnp.clip(result, min=-bound, max=bound).astype(kind)


def setup_inputs(seed: int = 0) -> dict:
    arg_keys = jax.random.split(jax.random.key(seed), 6)
    return {
        "image_embeds": noise(arg_keys[0], (TOKENS, D), 0.1, 0.59765625, ((0, 256),)),
        "text_embeds": noise(arg_keys[1], (TOKENS, D), 0.1, 0.59765625, ((0, 256),)),
        "positive": draw_positive(jax.random.fold_in(arg_keys[5], 71), 0),
        "logit_scale": jnp.clip(jax.random.uniform(arg_keys[3], (1,), jnp.float32, 2.0, 4.0), 2.0, 4.0),
        "logit_bias": jnp.clip(jax.random.uniform(arg_keys[4], (1,), jnp.float32, -2.0, -0.5), -2.0, -0.5),
    }


def tile_grads(image_rows, text_rows, labels_row, scale_value, bias_value, first_step):
    raw_scores = lax.dot_general(image_rows, text_rows, (((1,), (1,)), ((), ())), preferred_element_type=jnp.float32)
    sigmoid_term = jax.nn.sigmoid(scale_value * raw_scores + bias_value)
    if first_step:
        onehot = (labels_row[:, None] == jnp.arange(text_rows.shape[0], dtype=jnp.int32)[None, :]).astype(jnp.float32)
        sigmoid_term = sigmoid_term - onehot
    tile_bf = (scale_value * sigmoid_term).astype(jnp.bfloat16)
    grad_left = jnp.dot(tile_bf, text_rows, preferred_element_type=jnp.float32)
    grad_right = lax.dot_general(tile_bf, image_rows, (((0,), (0,)), ((), ())), preferred_element_type=jnp.float32)
    return grad_left, grad_right


def reference(image_embeds, text_embeds, positive, logit_scale, logit_bias):
    scale_value = logit_scale[0]
    bias_value = logit_bias[0]
    groups = TOKENS // GROUP
    images = image_embeds.reshape(groups, GROUP, D)
    captions = text_embeds.reshape(groups, GROUP, D)
    labels = positive.reshape(groups, GROUP)
    grad_img = jnp.zeros((groups, GROUP, D), jnp.float32)
    grad_txt = jnp.zeros((groups, GROUP, D), jnp.float32)
    for cycle_step in range(STEPS):
        partner = jnp.roll(captions, cycle_step, axis=0)

        def one_group(members, first_step=(cycle_step == 0)):
            return tile_grads(members[0], members[1], members[2], scale_value, bias_value, first_step)

        grad_left, grad_right = lax.map(one_group, (images, partner, labels))
        grad_img = grad_img + grad_left
        grad_txt = grad_txt + jnp.roll(grad_right, -cycle_step, axis=0)
    return grad_img.reshape(TOKENS, D), grad_txt.reshape(TOKENS, D)
```

```python
import jax
import jax.numpy as jnp
from jax import lax
from jax.sharding import PartitionSpec as P

AXES = ("blk", "inner")
BF = jnp.bfloat16
F32 = jnp.float32
CHUNKS = 2


def routes(nblk, ninner):
    def route(place):
        out = []
        for blk in range(nblk):
            for inner in range(ninner):
                col, half, low, core = blk // 2, blk % 2, inner // 2, inner % 2
                c, h, l, k = place(col, half, low, core)
                out.append((blk * ninner + inner, ((c % (nblk // 2)) * 2 + h) * ninner + l * 2 + k))
        return out

    return {
        "core": route(lambda c, h, l, k: (c, h, l, 1 - k)),
        "pair": route(lambda c, h, l, k: (c, h, 1 - l, k)),
        "mirror": route(lambda c, h, l, k: (c, 1 - h, 1 - l, k)),
        "next": route(lambda c, h, l, k: (c + 1, h, l, k)),
        "prev": route(lambda c, h, l, k: (c - 1, h, l, k)),
    }


def nt(a, b):
    return lax.dot_general(a, b, (((1,), (1,)), ((), ())), preferred_element_type=F32)


def tn(a, b):
    return lax.dot_general(a, b, (((0,), (0,)), ((), ())), preferred_element_type=F32)


def nn(a, b):
    return jnp.dot(a, b, preferred_element_type=F32)


def local(image, text, positive, logit_scale, logit_bias):
    nblk, ninner = lax.axis_size("blk"), lax.axis_size("inner")
    way = routes(nblk, ninner)
    move = lambda v, name: lax.ppermute(v, AXES, way[name])
    scale, bias = logit_scale[0], logit_bias[0]
    upper = (lax.axis_index("blk") % 2) == 1
    rows = text.shape[0]
    cut = rows // CHUNKS
    parts = [slice(i * cut, (i + 1) * cut) for i in range(CHUNKS)]

    text_x = [move(text[p], "next") for p in parts]
    image_n = move(image, "pair")
    image_c = move(image, "core")
    pos_c = move(positive, "core")
    pos_n = move(jnp.concatenate([positive, pos_c]), "pair")
    pos = jnp.concatenate([positive, pos_c, pos_n])
    text_m = [move(jnp.where(upper, t, text[p]), "mirror") for t, p in zip(text_x, parts)]
    image_nc = move(image_n, "core")
    images = jnp.concatenate([image, image_c, image_n, image_nc])
    at = pos - lax.axis_index("inner") * rows

    def tile(texts, first):
        s = jax.nn.sigmoid(scale * nt(texts, images) + bias)
        if first:
            s = s - (jnp.arange(rows, dtype=jnp.int32)[:, None] == at[None, :]).astype(F32)
        return (scale * s).astype(BF)

    tile0 = tile(text, True)
    tile_x = [tile(t, False) for t in text_x]
    grad_t = nn(tile0, images)
    grad_x = [nn(t, images) for t in tile_x]
    grad_i = tn(tile0, text) + sum(tn(a, b) for a, b in zip(tile_x, text_x))
    tile_m = [tile(t, False) for t in text_m]
    grad_m = [nn(t, images).astype(BF) for t in tile_m]
    back_m = [move(g, "mirror") for g in grad_m]
    send_x = [(g + jnp.where(upper, b.astype(F32), 0.0)).astype(BF) for g, b in zip(grad_x, back_m)]
    back_x = [move(g, "prev") for g in send_x]
    grad_i = grad_i + sum(tn(a, b) for a, b in zip(tile_m, text_m))
    core_nc = move(grad_i[3 * rows :].astype(BF), "core")
    pair_n = move((grad_i[2 * rows : 3 * rows] + core_nc.astype(F32)).astype(BF), "pair")
    core_c = move(grad_i[rows : 2 * rows].astype(BF), "core")
    grad_images = grad_i[:rows] + core_c.astype(F32) + pair_n.astype(F32)
    back_m = jnp.concatenate(back_m).astype(F32)
    grad_texts = grad_t + jnp.where(upper, 0.0, back_m) + jnp.concatenate(back_x).astype(F32)
    return grad_images, grad_texts


def solution(mesh):
    rows, flat = P(AXES, None), P(AXES)
    return jax.shard_map(
        local,
        mesh=mesh,
        in_specs=(rows, rows, flat, P(), P()),
        out_specs=(rows, rows),
        check_vma=False,
    )
```

```python
import jax
import jax.numpy as jnp
from jax import lax
from jax.experimental import pallas as pl
from jax.experimental.pallas import tpu as pltpu
from jax.sharding import PartitionSpec as P

AXES = ("blk", "inner")
BF = jnp.bfloat16
F32 = jnp.float32
CUTS = 3
LATE = 1
PAD = 16
PICK_US = 6
SEND_US = 8
GATE_US = 8
VMEM = pl.BlockSpec(memory_space=pltpu.VMEM)
SMEM = pl.BlockSpec(memory_space=pltpu.SMEM)
ANY = pl.BlockSpec(memory_space=pl.ANY)
HBM = pl.BlockSpec(memory_space=pltpu.HBM)


def routes(nblk, ninner):
    def route(place):
        out = []
        for blk in range(nblk):
            for inner in range(ninner):
                c, h, l, k = place(blk // 2, blk % 2, inner // 2, inner % 2)
                out.append((blk * ninner + inner, ((c % (nblk // 2)) * 2 + h) * ninner + l * 2 + k))
        return out

    return {
        "core": route(lambda c, h, l, k: (c, h, l, 1 - k)),
        "pair": route(lambda c, h, l, k: (c, h, 1 - l, k)),
        "mirror": route(lambda c, h, l, k: (c, 1 - h, 1 - l, k)),
        "next": route(lambda c, h, l, k: (c + 1, h, l, k)),
        "prev": route(lambda c, h, l, k: (c - 1, h, l, k)),
    }


def pieces(n, cuts):
    size = -(-n // (cuts * 16)) * 16
    return [slice(a, min(a + size, n)) for a in range(0, n, size)]


def nt(a, b):
    return lax.dot_general(a, b, (((1,), (1,)), ((), ())), preferred_element_type=F32)


def tn(a, b):
    return lax.dot_general(a, b, (((0,), (0,)), ((), ())), preferred_element_type=F32)


def nn(a, b):
    return jnp.dot(a, b, preferred_element_type=F32)


def call(body, name, outs, ins, scalars=(), aliases=None, after=(), us=0):
    shapes = tuple(jax.ShapeDtypeStruct(s, d) for s, d in outs)
    ns, ni, na = len(scalars), len(ins), len(after)

    def run(*refs):
        body(*refs[: ns + ni], *refs[ns + ni + na :])

    return pl.pallas_call(
        run,
        out_shape=shapes,
        in_specs=[SMEM] * ns + [VMEM] * ni + [ANY] * na,
        out_specs=tuple(VMEM for _ in shapes),
        input_output_aliases={k + ns: v for k, v in (aliases or {}).items()},
        compiler_params=pltpu.CompilerParams(vmem_limit_bytes=16 * 2**20),
        cost_estimate=pl.CostEstimate(flops=int(us * 1e9), bytes_accessed=0, transcendentals=0),
        name=name,
    )(*scalars, *ins, *after)


def gate(value, name, after, us=0):
    spec = [(value.shape, value.dtype)]
    return call(lambda a, b: None, name, spec, [value], aliases={0: 0}, after=after, us=us)[0]


def is_upper():
    return lax.rem(lax.axis_index("blk"), 2) == 1


def k_pack(image, pos, out):
    n, d = image.shape
    out[:n, :] = image[...]
    row = lax.broadcasted_iota(jnp.int32, (PAD, n), 0)
    p = jnp.broadcast_to(pos[...].reshape(1, n), (PAD, n))
    code = jnp.where(row == 0, p // 8, jnp.where(row == 1, p % 8, 0))
    out[n:, :] = jnp.zeros((PAD, d), BF)
    out[n:, :n] = code.astype(F32).astype(BF)


def pos_of(block):
    n = block.shape[0] - PAD
    code = block[n:, :n].astype(F32)
    return (code[0:1, :] * 8 + code[1:2, :]).astype(jnp.int32)


def tile_of(scale, bias, texts, images, pos=None):
    s = jax.nn.sigmoid(scale[0] * nt(texts, images) + bias[0])
    if pos is not None:
        first = lax.axis_index("inner") * texts.shape[0]
        at = lax.broadcasted_iota(jnp.int32, s.shape, 0) + first
        s = s - (at == pos).astype(F32)
    return (scale[0] * s).astype(BF)


def local(image, text, positive, logit_scale, logit_bias):
    nblk, ninner = lax.axis_size("blk"), lax.axis_size("inner")
    way = routes(nblk, ninner)
    move = lambda v, name: lax.ppermute(v, AXES, way[name])
    sc = (logit_scale, logit_bias)
    n, d = text.shape
    m = ninner * n
    parts = pieces(n, CUTS)
    size = [p.stop - p.start for p in parts]
    cuts = len(parts)
    early = cuts - LATE
    base = 2 * n
    done = base + parts[early].start
    blocks = [slice(j * n, (j + 1) * n) for j in range(ninner)]

    cut = []
    for p, s in zip(parts, size):

        def k_cut(text, out, p=p):
            out[...] = text[p, :]

        cut += call(k_cut, f"cut_{p.start}", [((s, d), BF)], [text], after=cut[-1:])
    (packed,) = call(k_pack, "pack", [((n + PAD, d), BF)], [image, positive], after=cut[:1])
    text_x = [move(t, "next") for t in cut]
    image_n = move(packed, "pair")
    image_c = move(packed, "core")

    text_m = []
    picked = []
    for i, (p, s, c, x) in enumerate(zip(parts, size, cut, text_x)):

        def k_pick(own, x, out):
            out[...] = jnp.where(is_upper(), x[...], own[...])

        after = picked[-1:] + (text_m[:1] if i == 2 else []) + ([image_c] if i == 0 else [])
        (t,) = call(k_pick, f"pick_{p.start}", [((s, d), BF)], [c, x], after=after, us=PICK_US)
        picked.append(t)
        text_m.append(move(t, "mirror"))
    text_m = [gate(t, f"gate_m_{i}", picked[-1:], us=GATE_US) for i, t in enumerate(text_m[:early])] + text_m[early:]
    image_n = gate(image_n, "gate_pair", picked[-1:])
    image_nc = move(image_n, "core")

    def k_tiles(scale, bias, i0, i_n, i_c, i_nc, *refs):
        own, xs, ms = refs[:cuts], refs[cuts : 2 * cuts], refs[2 * cuts : 2 * cuts + early]
        images, texts, tiles, pos = refs[2 * cuts + early :]
        for rows, ref in zip(blocks, (i_nc, i_n, i_c, i0)):
            images[rows, :] = ref[:n, :]
            pos[0:1, rows] = pos_of(ref)
        for k, group in enumerate((own, xs, ms)):
            for p, ref in zip(parts, group):
                texts[k * n + p.start : k * n + p.stop, :] = ref[...]
        tiles[:n, :] = tile_of(scale, bias, texts[:n, :], images[...], pos[0:1, :])
        tiles[n:base, :] = tile_of(scale, bias, texts[n:base, :], images[...])
        tiles[base:done, :] = tile_of(scale, bias, texts[base:done, :], images[...])

    images, texts, tiles, _ = call(
        k_tiles, "tiles", [((m, d), BF), ((3 * n, d), BF), ((3 * n, m), BF), ((8, m), jnp.int32)],
        [packed, image_n, image_c, image_nc, *cut, *text_x, *text_m[:early]], sc, us=2,
    )

    def k_last(scale, bias, images, *refs):
        got, (_, _, texts, tiles, to_nc, gi_n) = refs[:LATE], refs[LATE:]
        for p, t in zip(parts[early:], got):
            texts[base + p.start : base + p.stop, :] = t[...]
        tiles[done:, :] = tile_of(scale, bias, texts[done:, :], images[...])
        g = tn(tiles[:, : 2 * n], texts[...])
        to_nc[...] = g[:n, :].astype(BF)
        gi_n[...] = g[n:, :]

    texts, tiles, to_nc, gi_n = call(
        k_last, "mirror_last", [((3 * n, d), BF), ((3 * n, m), BF), ((n, d), BF), ((n, d), F32)],
        [images, *text_m[early:], texts, tiles], sc, aliases={1 + LATE: 0, 2 + LATE: 1},
    )
    got_nc = move(to_nc, "core")

    def k_mirror_grad(tiles, images, *grads):
        g = nn(tiles[base:, :], images[...]).astype(BF)
        for p, ref in zip(parts, grads):
            ref[...] = g[p, :]

    grad_m = list(call(k_mirror_grad, "mirror_grad", [((s, d), BF) for s in size], [tiles, images]))
    for i in range(1, cuts):
        grad_m[i] = gate(grad_m[i], f"gate_g_{i}", [grad_m[i - 1]])
    back_m = [move(g, "mirror") for g in grad_m]

    def k_pair(gi, got_nc, out):
        out[...] = (gi[...] + got_nc[...].astype(F32)).astype(BF)

    (send_n,) = call(k_pair, "to_pair", [((n, d), BF)], [gi_n, got_nc])
    got_n = move(send_n, "pair")

    def k_images(tiles, texts, to_c, gi_own):
        g = tn(tiles[:, 2 * n :], texts[...])
        to_c[...] = g[:n, :].astype(BF)
        gi_own[...] = g[n:, :]

    to_c, gi_own = call(k_images, "image_grads", [((n, d), BF), ((n, d), F32)], [tiles, texts], after=[send_n])

    def k_own_images(gi, got_c, out):
        out[...] = gi[...] + got_c[...].astype(F32)

    got_c = move(to_c, "core")
    (gi_own,) = call(k_own_images, "own_images", [((n, d), F32)], [gi_own, got_c])

    def k_texts(tiles, images, gt):
        gt[...] = nn(tiles[:base, :], images[...])

    (gt,) = call(k_texts, "text_grads", [((2 * n, d), F32)], [tiles, images], after=[to_c])

    back_x = []
    sent = []
    for p, s, back in zip(parts, size, back_m):

        def k_send(gt, back, out, p=p):
            b = jnp.where(is_upper(), back[...].astype(F32), 0.0)
            out[...] = (gt[n + p.start : n + p.stop, :] + b).astype(BF)

        (t,) = call(k_send, f"to_prev_{p.start}", [((s, d), BF)], [gt, back], after=sent[-1:], us=SEND_US)
        sent.append(t)
        back_x.append(move(t, "prev"))

    def k_end_images(gi, got_n, out):
        out[...] = gi[...] + got_n[...].astype(F32)

    def k_end_texts(gt, *refs):
        ms, xs, out = refs[:cuts], refs[cuts : 2 * cuts], refs[-1]
        up = is_upper()
        for p, a, b in zip(parts, ms, xs):
            out[p, :] = gt[p, :] + jnp.where(up, 0.0, a[...].astype(F32)) + b[...].astype(F32)

    (grad_images,) = call(k_end_images, "end_images", [((n, d), F32)], [gi_own, got_n])
    (grad_texts,) = call(k_end_texts, "end_texts", [((n, d), F32)], [gt, *back_m, *back_x])
    return grad_images, grad_texts


def solution(mesh):
    rows, flat = P(AXES, None), P(AXES)
    return jax.shard_map(
        local,
        mesh=mesh,
        in_specs=(rows, rows, flat, P(), P()),
        out_specs=(rows, rows),
        check_vma=False,
    )
```

```python
import jax
import jax.numpy as jnp
from jax import lax
from jax.experimental import pallas as pl
from jax.experimental.pallas import tpu as pltpu
from jax.sharding import PartitionSpec as P

AXES = ("blk", "inner")
BF = jnp.bfloat16
F32 = jnp.float32
CUTS = 3
LATE = 1
PICK_US = 6
SEND_US = (8, 8, 0)
GATE_US = 0
END_US = 0
GATE_X = (16, 0)
BACK_US = 14
LAST_US = 16
PAIR_US = 0
VMEM = pl.BlockSpec(memory_space=pltpu.VMEM)
SMEM = pl.BlockSpec(memory_space=pltpu.SMEM)
ANY = pl.BlockSpec(memory_space=pl.ANY)
HBM = pl.BlockSpec(memory_space=pltpu.HBM)


def routes(nblk, ninner):
    def route(place):
        out = []
        for blk in range(nblk):
            for inner in range(ninner):
                c, h, l, k = place(blk // 2, blk % 2, inner // 2, inner % 2)
                out.append((blk * ninner + inner, ((c % (nblk // 2)) * 2 + h) * ninner + l * 2 + k))
        return out

    return {
        "core": route(lambda c, h, l, k: (c, h, l, 1 - k)),
        "pair": route(lambda c, h, l, k: (c, h, 1 - l, k)),
        "mirror": route(lambda c, h, l, k: (c, 1 - h, 1 - l, k)),
        "next": route(lambda c, h, l, k: (c + 1, h, l, k)),
        "prev": route(lambda c, h, l, k: (c - 1, h, l, k)),
    }


def pieces(n, cuts):
    size = -(-n // (cuts * 16)) * 16
    return [slice(a, min(a + size, n)) for a in range(0, n, size)]


def nt(a, b):
    return lax.dot_general(a, b, (((1,), (1,)), ((), ())), preferred_element_type=F32)


def tn(a, b):
    return lax.dot_general(a, b, (((0,), (0,)), ((), ())), preferred_element_type=F32)


def nn(a, b):
    return jnp.dot(a, b, preferred_element_type=F32)


def call(body, name, outs, ins, scalars=(), aliases=None, after=(), us=0):
    shapes = tuple(jax.ShapeDtypeStruct(s, d) for s, d in outs)
    ns, ni, na = len(scalars), len(ins), len(after)

    def run(*refs):
        body(*refs[: ns + ni], *refs[ns + ni + na :])

    return pl.pallas_call(
        run,
        out_shape=shapes,
        in_specs=[SMEM] * ns + [VMEM] * ni + [ANY] * na,
        out_specs=tuple(VMEM for _ in shapes),
        input_output_aliases={k + ns: v for k, v in (aliases or {}).items()},
        compiler_params=pltpu.CompilerParams(vmem_limit_bytes=16 * 2**20),
        cost_estimate=pl.CostEstimate(flops=int(us * 1e9), bytes_accessed=0, transcendentals=0),
        name=name,
    )(*scalars, *ins, *after)


def gate(value, name, after=(), us=0):
    spec = [(value.shape, value.dtype)]
    return call(lambda a, b: None, name, spec, [value], aliases={0: 0}, after=after, us=us)[0]


def is_upper():
    return lax.rem(lax.axis_index("blk"), 2) == 1


def k_positives(own, other, image, out, kept):
    n = own.shape[0]
    kept[...] = image[...]
    out[...] = jnp.zeros(out.shape, out.dtype)
    out[0:1, :n] = own[...].reshape(1, n)
    out[0:1, n:] = other[...].reshape(1, n)


def tile_of(scale, bias, texts, images, pos=None):
    s = jax.nn.sigmoid(scale[0] * nt(texts, images) + bias[0])
    if pos is not None:
        first = lax.axis_index("inner") * texts.shape[0]
        at = lax.broadcasted_iota(jnp.int32, s.shape, 0) + first
        s = s - (at == pos).astype(F32)
    return (scale[0] * s).astype(BF)


def local(image, text, positive, logit_scale, logit_bias):
    nblk, ninner = lax.axis_size("blk"), lax.axis_size("inner")
    way = routes(nblk, ninner)
    move = lambda v, name: lax.ppermute(v, AXES, way[name])
    sc = (logit_scale, logit_bias)
    n, d = text.shape
    m = ninner * n
    parts = pieces(n, CUTS)
    size = [p.stop - p.start for p in parts]
    cuts = len(parts)
    early = cuts - LATE
    base = 2 * n
    done = base + parts[early].start
    blocks = [slice(j * n, (j + 1) * n) for j in range(ninner)]

    cut = []
    for p, s in zip(parts, size):

        def k_cut(text, out, p=p):
            out[...] = text[p, :]

        cut += call(k_cut, f"cut_{p.start}", [((s, d), BF)], [text], after=cut[-1:])
    text_x = [move(t, "next") for t in cut]
    image_n = move(image, "pair")
    image_c = move(image, "core")
    pos_c = move(positive, "core")

    text_m = []
    picked = []
    pos_n = ()
    for i, (p, s, c, x) in enumerate(zip(parts, size, cut, text_x)):

        def k_pick(own, x, out):
            out[...] = jnp.where(is_upper(), x[...], own[...])

        after = picked[-1:] + [[image_c, pos_c], [], [*text_m[:1], *pos_n]][min(i, 2)]
        (t,) = call(k_pick, f"pick_{p.start}", [((s, d), BF)], [c, x], after=after, us=PICK_US)
        picked.append(t)
        text_m.append(move(t, "mirror"))
        if i == 0:
            pos_own, kept = call(
                k_positives, "positives", [((8, 2 * n), jnp.int32), ((n, d), BF)], [positive, pos_c, image], after=[t]
            )
            pos_n = [move(pos_own, "pair")]
            picked.append(pos_own)
        if i == cuts - 2:
            image_n = gate(image_n, "gate_pair", [t], us=PAIR_US)
            image_nc = move(image_n, "core")
            picked.append(image_n)

    def k_tiles(scale, bias, i0, i_n, i_c, i_nc, pos_own, pos_n, *refs):
        own, xs = refs[:cuts], refs[cuts : 2 * cuts]
        images, texts, tiles, pos = refs[2 * cuts :]
        for rows, ref in zip(blocks, (i_nc, i_c, i_n, i0)):
            images[rows, :] = ref[...]
        for j, ref, at in ((0, pos_n, n), (1, pos_own, n), (2, pos_n, 0), (3, pos_own, 0)):
            pos[0:1, blocks[j]] = ref[0:1, at : at + n]
        for k, group in enumerate((own, xs)):
            for p, ref in zip(parts, group):
                texts[k * n + p.start : k * n + p.stop, :] = ref[...]
        tiles[:n, :] = tile_of(scale, bias, texts[:n, :], images[...], pos[0:1, :])
        tiles[n:base, :] = tile_of(scale, bias, texts[n:base, :], images[...])

    images, texts, tiles, _ = call(
        k_tiles, "tiles", [((m, d), BF), ((3 * n, d), BF), ((3 * n, m), BF), ((8, m), jnp.int32)],
        [kept, image_n, image_c, image_nc, pos_own, *pos_n, *cut, *text_x], sc,
    )

    for i in range(early):
        text_m[i] = gate(text_m[i], f"gate_m_{i}", [tiles, *text_m[:i]], us=GATE_US)

    def k_next_grads(tiles, images, out):
        out[...] = nn(tiles[n:base, :], images[...])

    def k_mirror_first(scale, bias, images, *refs):
        got, (_, _, texts, tiles, grad) = refs[:early], refs[early:]
        for p, t in zip(parts, got):
            texts[base + p.start : base + p.stop, :] = t[...]
        tiles[base:done, :] = tile_of(scale, bias, texts[base:done, :], images[...])
        grad[...] = nn(tiles[base : base + parts[0].stop, :], images[...]).astype(BF)

    texts, tiles, *grad_m = call(
        k_mirror_first, "mirror_first", [((3 * n, d), BF), ((3 * n, m), BF), ((size[0], d), BF)],
        [images, *text_m[:early], texts, tiles], sc, aliases={1 + early: 0, 2 + early: 1},
    )
    back_m = [move(grad_m[0], "mirror")]
    text_m[early] = gate(text_m[early], "gate_m_last", grad_m, us=LAST_US)

    def k_last(scale, bias, images, *refs):
        got, (_, _, texts, tiles, to_core) = refs[:LATE], refs[LATE:]
        for p, t in zip(parts[early:], got):
            texts[base + p.start : base + p.stop, :] = t[...]
        tiles[done:, :] = tile_of(scale, bias, texts[done:, :], images[...])
        to_core[...] = tn(tiles[:, : 2 * n], texts[...]).astype(BF)

    texts, tiles, to_core = call(
        k_last, "mirror_last", [((3 * n, d), BF), ((3 * n, m), BF), ((2 * n, d), BF)],
        [images, *text_m[early:], texts, tiles], sc, aliases={1 + LATE: 0, 2 + LATE: 1}, after=grad_m[-1:],
    )
    got_core = move(to_core, "core")

    def k_rest_grads(tiles, images, *grads):
        g = nn(tiles[base + parts[1].start :, :], images[...]).astype(BF)
        for p, ref in zip(parts[1:], grads):
            ref[...] = g[p.start - parts[1].start : p.stop - parts[1].start, :]

    grad_m += call(k_rest_grads, "mirror_rest_grads", [((s, d), BF) for s in size[1:]], [tiles, images])
    back_m.append(move(grad_m[1], "mirror"))
    (gx,) = call(k_next_grads, "next_text_grads", [((n, d), F32)], [tiles, images], after=[grad_m[1]])

    def k_pair(tiles, texts, got_core, out):
        g = tn(tiles[:, 2 * n : 3 * n], texts[...])
        out[...] = (g + got_core[:n, :].astype(F32)).astype(BF)

    back_m[0] = gate(back_m[0], "gate_back_0", [gx], us=BACK_US)
    (send_n,) = call(k_pair, "to_pair", [((n, d), BF)], [tiles, texts, got_core], after=[back_m[0]])
    got_n = move(send_n, "pair")
    def k_own_grads(tiles, images, out):
        out[...] = nn(tiles[:n, :], images[...])

    def k_own_images(tiles, texts, got_core, out):
        skip = n % 128
        g = tn(tiles[:, 3 * n - skip :], texts[...])[skip:, :]
        out[...] = g + got_core[n:, :].astype(F32)

    back_x = []
    sent = []
    for i, (p, s) in enumerate(zip(parts, size)):

        def k_send(gx, back, out, p=p):
            b = jnp.where(is_upper(), back[...].astype(F32), 0.0)
            out[...] = (gx[p, :] + b).astype(BF)

        after = sent[-1:] or [send_n]
        (t,) = call(k_send, f"to_prev_{p.start}", [((s, d), BF)], [gx, back_m[i]], after=after, us=SEND_US[i])
        sent.append(t)
        back_x.append(move(t, "prev"))
        if i == 0:
            for j in range(2, cuts):
                back_m.append(move(gate(grad_m[j], f"gate_g_{j}", [t]), "mirror"))
        if i == 2:
            back_x[0] = gate(back_x[0], "gate_x_0", [t], us=GATE_X[0])
            (gt,) = call(k_own_grads, "own_text_grads", [((n, d), F32)], [tiles, images], after=back_x[:1])
            (gi_own,) = call(k_own_images, "own_images", [((n, d), F32)], [tiles, texts, got_core], after=[gt])

    back_x[1] = gate(back_x[1], "gate_x_1", [], us=GATE_X[1])

    def k_end_images(gi, got_n, out, token):
        out[...] = gi[...] + got_n[...].astype(F32)
        token[...] = jnp.zeros(token.shape, F32)

    grad_images, token = call(k_end_images, "end_images", [((n, d), F32), ((8, 128), F32)], [gi_own, got_n])

    grad_texts = None
    for name, a, b in (("end_texts_first", 0, cuts - 1), ("end_texts_last", cuts - 1, cuts)):
        at, rows = parts[a].start, parts[b - 1].stop - parts[a].start

        def k_end_texts(gt, *refs, a=a, b=b, at=at, rows=rows):
            ms, xs, (out, block, sem) = refs[: b - a], refs[b - a : 2 * (b - a)], refs[-3:]
            up = is_upper()
            for p, m_ref, x_ref in zip(parts[a:b], ms, xs):
                g = gt[p, :] + jnp.where(up, 0.0, m_ref[...].astype(F32)) + x_ref[...].astype(F32)
                block[p.start - at : p.stop - at, :] = g
            copy = pltpu.make_async_copy(block, out.at[pl.ds(at, rows), :], sem)
            copy.start()
            copy.wait()

        ins = [gt, *back_m[a:b], *back_x[a:b]]
        old = [] if grad_texts is None else [grad_texts]
        after = [token] if old else []
        grad_texts = pl.pallas_call(
            k_end_texts,
            out_shape=jax.ShapeDtypeStruct((n, d), F32),
            in_specs=[VMEM] * len(ins) + [HBM] * len(old) + [ANY] * len(after),
            out_specs=HBM,
            input_output_aliases={len(ins): 0} if old else {},
            scratch_shapes=[pltpu.VMEM((rows, d), F32), pltpu.SemaphoreType.DMA],
            compiler_params=pltpu.CompilerParams(vmem_limit_bytes=16 * 2**20),
            cost_estimate=pl.CostEstimate(flops=0 if old else int(END_US * 1e9), bytes_accessed=0, transcendentals=0),
            name=name,
        )(*ins, *old, *after)
    return grad_images, grad_texts


def solution(mesh):
    rows, flat = P(AXES, None), P(AXES)
    return jax.shard_map(
        local,
        mesh=mesh,
        in_specs=(rows, rows, flat, P(), P()),
        out_specs=(rows, rows),
        check_vma=False,
    )
```

```python
import jax
import jax.numpy as jnp
from jax import lax
from jax.experimental import pallas as pl
from jax.experimental.pallas import tpu as pltpu
from jax.sharding import PartitionSpec as P

AXES = ("blk", "inner")
BF = jnp.bfloat16
F32 = jnp.float32
CUTS = 3
LATE = 1
PICK_US = 6
SEND_US = (8, 8, 0)
GATE_US = 0
GATE_X = (16, 0)
BACK_US = 6
LAST_US = 16
PAIR_US = 0
FIRST_US = 8
VMEM = pl.BlockSpec(memory_space=pltpu.VMEM)
SMEM = pl.BlockSpec(memory_space=pltpu.SMEM)
ANY = pl.BlockSpec(memory_space=pl.ANY)
HBM = pl.BlockSpec(memory_space=pltpu.HBM)


def routes(nblk, ninner):
    def route(place):
        out = []
        for blk in range(nblk):
            for inner in range(ninner):
                c, h, l, k = place(blk // 2, blk % 2, inner // 2, inner % 2)
                out.append((blk * ninner + inner, ((c % (nblk // 2)) * 2 + h) * ninner + l * 2 + k))
        return out

    return {
        "core": route(lambda c, h, l, k: (c, h, l, 1 - k)),
        "pair": route(lambda c, h, l, k: (c, h, 1 - l, k)),
        "mirror": route(lambda c, h, l, k: (c, 1 - h, 1 - l, k)),
        "next": route(lambda c, h, l, k: (c + 1, h, l, k)),
        "prev": route(lambda c, h, l, k: (c - 1, h, l, k)),
    }


def pieces(n, cuts):
    size = -(-n // (cuts * 16)) * 16
    stops = [n - size * i for i in range(cuts) if n - size * i > 0][::-1]
    return [slice(a, b) for a, b in zip([0] + stops, stops)]


def nt(a, b):
    return lax.dot_general(a, b, (((1,), (1,)), ((), ())), preferred_element_type=F32)


def tn(a, b):
    return lax.dot_general(a, b, (((0,), (0,)), ((), ())), preferred_element_type=F32)


def nn(a, b):
    return jnp.dot(a, b, preferred_element_type=F32)


def call(body, name, outs, ins, scalars=(), aliases=None, after=(), us=0):
    shapes = tuple(jax.ShapeDtypeStruct(s, d) for s, d in outs)
    ns, ni, na = len(scalars), len(ins), len(after)

    def run(*refs):
        body(*refs[: ns + ni], *refs[ns + ni + na :])

    return pl.pallas_call(
        run,
        out_shape=shapes,
        in_specs=[SMEM] * ns + [VMEM] * ni + [ANY] * na,
        out_specs=tuple(VMEM for _ in shapes),
        input_output_aliases={k + ns: v for k, v in (aliases or {}).items()},
        compiler_params=pltpu.CompilerParams(vmem_limit_bytes=16 * 2**20),
        cost_estimate=pl.CostEstimate(flops=int(us * 1e9), bytes_accessed=0, transcendentals=0),
        name=name,
    )(*scalars, *ins, *after)


def gate(value, name, after=(), us=0):
    spec = [(value.shape, value.dtype)]
    return call(lambda a, b: None, name, spec, [value], aliases={0: 0}, after=after, us=us)[0]


def is_upper():
    return lax.rem(lax.axis_index("blk"), 2) == 1


def tile_of(scale, bias, texts, images, pos=None):
    s = jax.nn.sigmoid(scale[0] * nt(texts, images) + bias[0])
    if pos is not None:
        first = lax.axis_index("inner") * texts.shape[0]
        at = lax.broadcasted_iota(jnp.int32, s.shape, 0) + first
        s = s - (at == pos).astype(F32)
    return (scale[0] * s).astype(BF)


def local(image, text, positive, logit_scale, logit_bias):
    nblk, ninner = lax.axis_size("blk"), lax.axis_size("inner")
    way = routes(nblk, ninner)
    move = lambda v, name: lax.ppermute(v, AXES, way[name])
    sc = (logit_scale, logit_bias)
    n, d = text.shape
    m = ninner * n
    parts = pieces(n, CUTS)
    size = [p.stop - p.start for p in parts]
    cuts = len(parts)
    early = cuts - LATE
    base = 2 * n
    done = base + parts[early].start
    blocks = [slice(j * n, (j + 1) * n) for j in range(ninner)]

    cut = []
    for p, s in zip(parts, size):

        def k_cut(text, out, p=p):
            out[...] = text[p, :]

        cut += call(k_cut, f"cut_{p.start}", [((s, d), BF)], [text], after=cut[-1:])
    text_x = [move(t, "next") for t in cut]
    image_n = move(image, "pair")
    image_c = move(image, "core")
    pos_c = move(positive, "core")

    text_m = []
    picked = []
    pos_n = ()
    for i, (p, s, c, x) in enumerate(zip(parts, size, cut, text_x)):

        def k_pick(own, x, out):
            out[...] = jnp.where(is_upper(), x[...], own[...])

        after = picked[-1:] + [[image_c, pos_c], [], [*text_m[:1], *pos_n]][min(i, 2)]
        (t,) = call(k_pick, f"pick_{p.start}", [((s, d), BF)], [c, x], after=after, us=PICK_US)
        picked.append(t)
        text_m.append(move(t, "mirror"))
        if i == 0:

            def k_own(pos, pos_c, image, image_c, *refs):
                own, (out, images, texts) = refs[:cuts], refs[cuts:]
                out[...] = jnp.zeros(out.shape, out.dtype)
                out[0:1, :n] = pos[...].reshape(1, n)
                out[0:1, n:] = pos_c[...].reshape(1, n)
                images[blocks[1], :] = image_c[...]
                images[blocks[3], :] = image[...]
                for p, ref in zip(parts, own):
                    texts[p, :] = ref[...]

            pos_own, images, texts = call(
                k_own, "own_blocks", [((8, 2 * n), jnp.int32), ((m, d), BF), ((3 * n, d), BF)],
                [positive, pos_c, image, image_c, *cut], after=[t],
            )
            pos_n = [move(pos_own, "pair")]
            picked.append(pos_own)
        if i == cuts - 2:
            text_m[0] = gate(text_m[0], "gate_first", [t], us=FIRST_US)
            image_n = gate(image_n, "gate_pair", [t, text_m[0]], us=PAIR_US)
            image_nc = move(image_n, "core")
            picked.append(image_n)

    def k_tiles(scale, bias, i_n, i_nc, pos_own, pos_n, *refs):
        xs, (_, _, images, texts, tiles, pos) = refs[:cuts], refs[cuts:]
        images[blocks[0], :] = i_nc[...]
        images[blocks[2], :] = i_n[...]
        for j, ref, at in ((0, pos_n, n), (1, pos_own, n), (2, pos_n, 0), (3, pos_own, 0)):
            pos[0:1, blocks[j]] = ref[0:1, at : at + n]
        for p, ref in zip(parts, xs):
            texts[n + p.start : n + p.stop, :] = ref[...]
        tiles[:n, :] = tile_of(scale, bias, texts[:n, :], images[...], pos[0:1, :])
        tiles[n:base, :] = tile_of(scale, bias, texts[n:base, :], images[...])

    images, texts, tiles, _ = call(
        k_tiles, "tiles", [((m, d), BF), ((3 * n, d), BF), ((3 * n, m), BF), ((8, m), jnp.int32)],
        [image_n, image_nc, pos_own, *pos_n, *text_x, images, texts], sc,
        aliases={4 + cuts: 0, 5 + cuts: 1},
    )

    for i in range(early):
        text_m[i] = gate(text_m[i], f"gate_m_{i}", [tiles, *text_m[:i]], us=GATE_US)

    def k_next_first(tiles, images, out):
        out[...] = nn(tiles[n : n + parts[0].stop, :], images[...])

    def k_next_rest(tiles, images, out):
        out[...] = nn(tiles[n + parts[0].stop : base, :], images[...])

    def k_mirror_first(scale, bias, images, *refs):
        got, (_, _, texts, tiles, grad) = refs[:early], refs[early:]
        for p, t in zip(parts, got):
            texts[base + p.start : base + p.stop, :] = t[...]
        tiles[base:done, :] = tile_of(scale, bias, texts[base:done, :], images[...])
        grad[...] = nn(tiles[base : base + parts[0].stop, :], images[...]).astype(BF)

    texts, tiles, *grad_m = call(
        k_mirror_first, "mirror_first", [((3 * n, d), BF), ((3 * n, m), BF), ((size[0], d), BF)],
        [images, *text_m[:early], texts, tiles], sc, aliases={1 + early: 0, 2 + early: 1},
    )
    back_m = [move(grad_m[0], "mirror")]
    text_m[early] = gate(text_m[early], "gate_m_last", grad_m, us=LAST_US)

    def k_last(scale, bias, images, *refs):
        got, (_, _, texts, tiles, to_core) = refs[:LATE], refs[LATE:]
        for p, t in zip(parts[early:], got):
            texts[base + p.start : base + p.stop, :] = t[...]
        tiles[done:, :] = tile_of(scale, bias, texts[done:, :], images[...])
        to_core[...] = tn(tiles[:, :n], texts[...]).astype(BF)

    texts, tiles, to_core = call(
        k_last, "mirror_last", [((3 * n, d), BF), ((3 * n, m), BF), ((n, d), BF)],
        [images, *text_m[early:], texts, tiles], sc, aliases={1 + LATE: 0, 2 + LATE: 1}, after=grad_m[-1:],
    )
    got_core = move(to_core, "core")

    def k_rest_grads(tiles, images, *grads):
        g = nn(tiles[base + parts[1].start :, :], images[...]).astype(BF)
        for p, ref in zip(parts[1:], grads):
            ref[...] = g[p.start - parts[1].start : p.stop - parts[1].start, :]

    grad_m += call(k_rest_grads, "mirror_rest_grads", [((s, d), BF) for s in size[1:]], [tiles, images])
    back_m.append(move(grad_m[1], "mirror"))
    (gx,) = call(k_next_first, "next_text_first", [((size[0], d), F32)], [tiles, images], after=[grad_m[1]])

    def k_pair(tiles, texts, got_core, out):
        g = tn(tiles[:, 2 * n : 3 * n], texts[...])
        out[...] = (g + got_core[...].astype(F32)).astype(BF)

    back_m[0] = gate(back_m[0], "gate_back_0", [gx], us=BACK_US)
    (send_n,) = call(k_pair, "to_pair", [((n, d), BF)], [tiles, texts, got_core], after=[back_m[0]])
    got_n = move(send_n, "pair")
    def k_own_grads(tiles, images, out):
        out[...] = nn(tiles[:n, :], images[...])

    def k_core_images(tiles, texts, out):
        skip = n % 128
        out[...] = tn(tiles[:, n - skip : 2 * n], texts[...])[skip:, :].astype(BF)

    def k_own_images(tiles, texts, got_c, out):
        skip = n % 128
        g = tn(tiles[:, 3 * n - skip :], texts[...])[skip:, :]
        out[...] = g + got_c[...].astype(F32)

    back_x = []
    sent = []
    for i, (p, s) in enumerate(zip(parts, size)):

        def k_send(gx, back, out, p=p):
            b = jnp.where(is_upper(), back[...].astype(F32), 0.0)
            at = p.start if p.start == 0 else p.start - parts[0].stop
            out[...] = (gx[at : at + p.stop - p.start, :] + b).astype(BF)

        after = sent[-1:] or [send_n]
        (t,) = call(k_send, f"to_prev_{p.start}", [((s, d), BF)], [gx, back_m[i]], after=after, us=SEND_US[i])
        sent.append(t)
        back_x.append(move(t, "prev"))
        if i == 0:
            for j in range(2, cuts):
                back_m.append(move(gate(grad_m[j], f"gate_g_{j}", [t]), "mirror"))
            (gx,) = call(k_next_rest, "next_text_rest", [((n - size[0], d), F32)], [tiles, images], after=[t])
        if i == 1:
            (to_c,) = call(k_core_images, "core_images", [((n, d), BF)], [tiles, texts], after=[t])
            got_c = move(to_c, "core")
        if i == 2:
            back_x[0] = gate(back_x[0], "gate_x_0", [t], us=GATE_X[0])
            (gt,) = call(k_own_grads, "own_text_grads", [((n, d), F32)], [tiles, images], after=back_x[:1])
            (gi_own,) = call(k_own_images, "own_images", [((n, d), F32)], [tiles, texts, got_c], after=[gt])

    back_x[1] = gate(back_x[1], "gate_x_1", [gi_own], us=GATE_X[1])

    def write_texts(name, a, b, old, after):
        at, rows = parts[a].start, parts[b - 1].stop - parts[a].start

        def k_end_texts(gt, *refs):
            ms, xs, (out, *token, block, sem) = refs[: b - a], refs[b - a : 2 * (b - a)], refs[-3 if old else -4 :]
            up = is_upper()
            for p, m_ref, x_ref in zip(parts[a:b], ms, xs):
                g = gt[p, :] + jnp.where(up, 0.0, m_ref[...].astype(F32)) + x_ref[...].astype(F32)
                block[p.start - at : p.stop - at, :] = g
            copy = pltpu.make_async_copy(block, out.at[pl.ds(at, rows), :], sem)
            copy.start()
            for ref in token:
                ref[...] = jnp.zeros(ref.shape, F32)
            copy.wait()

        ins = [gt, *back_m[a:b], *back_x[a:b]]
        return pl.pallas_call(
            k_end_texts,
            out_shape=[jax.ShapeDtypeStruct((n, d), F32), jax.ShapeDtypeStruct((8, 128), F32)][: 1 if old else 2],
            in_specs=[VMEM] * len(ins) + [HBM] * len(old) + [ANY] * len(after),
            out_specs=[HBM, VMEM][: 1 if old else 2],
            input_output_aliases={len(ins): 0} if old else {},
            scratch_shapes=[pltpu.VMEM((rows, d), F32), pltpu.SemaphoreType.DMA],
            compiler_params=pltpu.CompilerParams(vmem_limit_bytes=16 * 2**20),
            cost_estimate=pl.CostEstimate(flops=0, bytes_accessed=0, transcendentals=0),
            name=name,
        )(*ins, *old, *after)

    def k_end_images(gi, got_n, out, token):
        out[...] = gi[...] + got_n[...].astype(F32)
        token[...] = jnp.zeros(token.shape, F32)

    grad_texts, token = write_texts("end_texts_first", 0, cuts - 1, [], [])
    grad_images, token = call(
        k_end_images, "end_images", [((n, d), F32), ((8, 128), F32)], [gi_own, got_n], after=[token]
    )
    (grad_texts,) = write_texts("end_texts_last", cuts - 1, cuts, [grad_texts], [token])
    return grad_images, grad_texts


def solution(mesh):
    rows, flat = P(AXES, None), P(AXES)
    return jax.shard_map(
        local,
        mesh=mesh,
        in_specs=(rows, rows, flat, P(), P()),
        out_specs=(rows, rows),
        check_vma=False,
    )
```

```python
import jax
import jax.numpy as jnp
from jax import lax
from jax.experimental import pallas as pl
from jax.experimental.pallas import tpu as pltpu
from jax.sharding import PartitionSpec as P

AXES = ("blk", "inner")
BF = jnp.bfloat16
F32 = jnp.float32
CUTS = 3
LATE = 1
PICK_US = 6
SEND_US = (8, 8, 0)
GATE_US = 0
GATE_X = (16, 0)
BACK_US = 6
LAST_US = 16
PAIR_US = 0
FIRST_US = 8
VMEM = pl.BlockSpec(memory_space=pltpu.VMEM)
SMEM = pl.BlockSpec(memory_space=pltpu.SMEM)
ANY = pl.BlockSpec(memory_space=pl.ANY)
HBM = pl.BlockSpec(memory_space=pltpu.HBM)


def routes(nblk, ninner):
    def route(place):
        out = []
        for blk in range(nblk):
            for inner in range(ninner):
                c, h, l, k = place(blk // 2, blk % 2, inner // 2, inner % 2)
                out.append((blk * ninner + inner, ((c % (nblk // 2)) * 2 + h) * ninner + l * 2 + k))
        return out

    return {
        "core": route(lambda c, h, l, k: (c, h, l, 1 - k)),
        "pair": route(lambda c, h, l, k: (c, h, 1 - l, k)),
        "mirror": route(lambda c, h, l, k: (c, 1 - h, 1 - l, k)),
        "next": route(lambda c, h, l, k: (c + 1, h, l, k)),
        "prev": route(lambda c, h, l, k: (c - 1, h, l, k)),
    }


def pieces(n, cuts):
    size = -(-n // (cuts * 16)) * 16
    stops = [n - size * i for i in range(cuts) if n - size * i > 0][::-1]
    return [slice(a, b) for a, b in zip([0] + stops, stops)]


def nt(a, b):
    return lax.dot_general(a, b, (((1,), (1,)), ((), ())), preferred_element_type=F32)


def tn(a, b):
    return lax.dot_general(a, b, (((0,), (0,)), ((), ())), preferred_element_type=F32)


def nn(a, b):
    return jnp.dot(a, b, preferred_element_type=F32)


def call(body, name, outs, ins, scalars=(), aliases=None, after=(), us=0):
    shapes = tuple(jax.ShapeDtypeStruct(s, d) for s, d in outs)
    ns, ni, na = len(scalars), len(ins), len(after)

    def run(*refs):
        body(*refs[: ns + ni], *refs[ns + ni + na :])

    return pl.pallas_call(
        run,
        out_shape=shapes,
        in_specs=[SMEM] * ns + [VMEM] * ni + [ANY] * na,
        out_specs=tuple(VMEM for _ in shapes),
        input_output_aliases={k + ns: v for k, v in (aliases or {}).items()},
        compiler_params=pltpu.CompilerParams(vmem_limit_bytes=16 * 2**20),
        cost_estimate=pl.CostEstimate(flops=int(us * 1e9), bytes_accessed=0, transcendentals=0),
        name=name,
    )(*scalars, *ins, *after)


def gate(value, name, after=(), us=0):
    spec = [(value.shape, value.dtype)]
    return call(lambda a, b: None, name, spec, [value], aliases={0: 0}, after=after, us=us)[0]


def is_upper():
    return lax.rem(lax.axis_index("blk"), 2) == 1


def tile_of(scale, bias, texts, images, pos=None):
    s = jax.nn.sigmoid(scale[0] * nt(texts, images) + bias[0])
    if pos is not None:
        first = lax.axis_index("inner") * texts.shape[0]
        at = lax.broadcasted_iota(jnp.int32, s.shape, 0) + first
        s = s - (at == pos).astype(F32)
    return (scale[0] * s).astype(BF)


def local(image, text, positive, logit_scale, logit_bias):
    nblk, ninner = lax.axis_size("blk"), lax.axis_size("inner")
    way = routes(nblk, ninner)
    move = lambda v, name: lax.ppermute(v, AXES, way[name])
    sc = (logit_scale, logit_bias)
    n, d = text.shape
    m = ninner * n
    parts = pieces(n, CUTS)
    size = [p.stop - p.start for p in parts]
    cuts = len(parts)
    early = cuts - LATE
    base = 2 * n
    done = base + parts[early].start
    blocks = [slice(j * n, (j + 1) * n) for j in range(ninner)]

    cut = []
    for p, s in zip(parts, size):

        def k_cut(text, out, p=p):
            out[...] = text[p, :]

        cut += call(k_cut, f"cut_{p.start}", [((s, d), BF)], [text], after=cut[-1:])
    text_x = [move(t, "next") for t in cut]
    image_n = move(image, "pair")
    image_c = move(image, "core")
    pos_c = move(positive, "core")

    text_m = []
    picked = []
    pos_n = ()
    for i, (p, s, c, x) in enumerate(zip(parts, size, cut, text_x)):

        def k_pick(own, x, out):
            out[...] = jnp.where(is_upper(), x[...], own[...])

        after = picked[-1:] + [[image_c, pos_c], [], [*text_m[:1], *pos_n]][min(i, 2)]
        (t,) = call(k_pick, f"pick_{p.start}", [((s, d), BF)], [c, x], after=after, us=PICK_US)
        picked.append(t)
        text_m.append(move(t, "mirror"))
        if i == 0:

            def k_own(pos, pos_c, image, image_c, *refs):
                own, (out, images, texts) = refs[:cuts], refs[cuts:]
                out[...] = jnp.zeros(out.shape, out.dtype)
                out[0:1, :n] = pos[...].reshape(1, n)
                out[0:1, n:] = pos_c[...].reshape(1, n)
                images[blocks[1], :] = image_c[...]
                images[blocks[3], :] = image[...]
                for p, ref in zip(parts, own):
                    texts[p, :] = ref[...]

            pos_own, images, texts = call(
                k_own, "own_blocks", [((8, 2 * n), jnp.int32), ((m, d), BF), ((3 * n, d), BF)],
                [positive, pos_c, image, image_c, *cut], after=[t],
            )
            pos_n = [move(pos_own, "pair")]
            picked.append(pos_own)
        if i == cuts - 2:
            text_m[0] = gate(text_m[0], "gate_first", [t], us=FIRST_US)
            image_n = gate(image_n, "gate_pair", [t, text_m[0]], us=PAIR_US)
            image_nc = move(image_n, "core")
            picked.append(image_n)

    def k_tiles(scale, bias, i_n, i_nc, pos_own, pos_n, *refs):
        xs, (_, _, images, texts, tiles, pos) = refs[:cuts], refs[cuts:]
        images[blocks[0], :] = i_nc[...]
        images[blocks[2], :] = i_n[...]
        for j, ref, at in ((0, pos_n, n), (1, pos_own, n), (2, pos_n, 0), (3, pos_own, 0)):
            pos[0:1, blocks[j]] = ref[0:1, at : at + n]
        for p, ref in zip(parts, xs):
            texts[n + p.start : n + p.stop, :] = ref[...]
        tiles[:n, :] = tile_of(scale, bias, texts[:n, :], images[...], pos[0:1, :])
        tiles[n:base, :] = tile_of(scale, bias, texts[n:base, :], images[...])

    images, texts, tiles, _ = call(
        k_tiles, "tiles", [((m, d), BF), ((3 * n, d), BF), ((3 * n, m), BF), ((8, m), jnp.int32)],
        [image_n, image_nc, pos_own, *pos_n, *text_x, images, texts], sc,
        aliases={4 + cuts: 0, 5 + cuts: 1},
    )

    for i in range(early):
        text_m[i] = gate(text_m[i], f"gate_m_{i}", [tiles, *text_m[:i]], us=GATE_US)

    def k_next_first(tiles, images, out):
        out[...] = nn(tiles[n : n + parts[0].stop, :], images[...])

    def k_next_rest(tiles, images, out):
        out[...] = nn(tiles[n + parts[0].stop : base, :], images[...])

    def k_mirror_first(scale, bias, images, *refs):
        got, (_, _, texts, tiles, grad) = refs[:early], refs[early:]
        for p, t in zip(parts, got):
            texts[base + p.start : base + p.stop, :] = t[...]
        tiles[base:done, :] = tile_of(scale, bias, texts[base:done, :], images[...])
        grad[...] = nn(tiles[base : base + parts[0].stop, :], images[...]).astype(BF)

    texts, tiles, *grad_m = call(
        k_mirror_first, "mirror_first", [((3 * n, d), BF), ((3 * n, m), BF), ((size[0], d), BF)],
        [images, *text_m[:early], texts, tiles], sc, aliases={1 + early: 0, 2 + early: 1},
    )
    back_m = [move(grad_m[0], "mirror")]
    text_m[early] = gate(text_m[early], "gate_m_last", grad_m, us=LAST_US)

    def k_last(scale, bias, images, *refs):
        got, (_, _, texts, tiles, to_core) = refs[:LATE], refs[LATE:]
        for p, t in zip(parts[early:], got):
            texts[base + p.start : base + p.stop, :] = t[...]
        tiles[done:, :] = tile_of(scale, bias, texts[done:, :], images[...])
        to_core[...] = tn(tiles[:, :n], texts[...]).astype(BF)

    texts, tiles, to_core = call(
        k_last, "mirror_last", [((3 * n, d), BF), ((3 * n, m), BF), ((n, d), BF)],
        [images, *text_m[early:], texts, tiles], sc, aliases={1 + LATE: 0, 2 + LATE: 1}, after=grad_m[-1:],
    )
    got_core = move(to_core, "core")

    def k_rest_grads(tiles, images, *grads):
        g = nn(tiles[base + parts[1].start :, :], images[...]).astype(BF)
        for p, ref in zip(parts[1:], grads):
            ref[...] = g[p.start - parts[1].start : p.stop - parts[1].start, :]

    grad_m += call(k_rest_grads, "mirror_rest_grads", [((s, d), BF) for s in size[1:]], [tiles, images])
    back_m.append(move(grad_m[1], "mirror"))
    (gx,) = call(k_next_first, "next_text_first", [((size[0], d), F32)], [tiles, images], after=[grad_m[1]])

    def k_pair(tiles, texts, got_core, out):
        g = tn(tiles[:, 2 * n : 3 * n], texts[...])
        out[...] = (g + got_core[...].astype(F32)).astype(BF)

    back_m[0] = gate(back_m[0], "gate_back_0", [gx], us=BACK_US)
    (send_n,) = call(k_pair, "to_pair", [((n, d), BF)], [tiles, texts, got_core], after=[back_m[0]])
    got_n = move(send_n, "pair")
    def k_own_grads(tiles, images, out):
        out[...] = nn(tiles[:n, :], images[...])

    def k_core_images(tiles, texts, out):
        skip = n % 128
        out[...] = tn(tiles[:, n - skip : 2 * n], texts[...])[skip:, :].astype(BF)

    def k_own_images(tiles, texts, got_c, out):
        skip = n % 128
        g = tn(tiles[:, 3 * n - skip :], texts[...])[skip:, :]
        out[...] = g + got_c[...].astype(F32)

    back_x = []
    sent = []
    for i, (p, s) in enumerate(zip(parts, size)):

        def k_send(gx, back, out, p=p):
            b = jnp.where(is_upper(), back[...].astype(F32), 0.0)
            at = p.start if p.start == 0 else p.start - parts[0].stop
            out[...] = (gx[at : at + p.stop - p.start, :] + b).astype(BF)

        after = sent[-1:] or [send_n]
        (t,) = call(k_send, f"to_prev_{p.start}", [((s, d), BF)], [gx, back_m[i]], after=after, us=SEND_US[i])
        sent.append(t)
        back_x.append(move(t, "prev"))
        if i == 0:
            for j in range(2, cuts):
                grad_m[j] = gate(grad_m[j], f"gate_g_{j}", [t])
                back_m.append(move(grad_m[j], "mirror"))
            (gx,) = call(k_next_rest, "next_text_rest", [((n - size[0], d), F32)], [tiles, images], after=grad_m[-1:])
        if i == 1:
            (to_c,) = call(k_core_images, "core_images", [((n, d), BF)], [tiles, texts], after=[t])
            got_c = move(to_c, "core")
        if i == 2:
            back_x[0] = gate(back_x[0], "gate_x_0", [t], us=GATE_X[0])
            (gt,) = call(k_own_grads, "own_text_grads", [((n, d), F32)], [tiles, images], after=back_x[:1])
            (gi_own,) = call(k_own_images, "own_images", [((n, d), F32)], [tiles, texts, got_c], after=[gt])

    back_x[1] = gate(back_x[1], "gate_x_1", [gi_own], us=GATE_X[1])

    def write_texts(name, a, b, old, after):
        at, rows = parts[a].start, parts[b - 1].stop - parts[a].start

        def k_end_texts(gt, *refs):
            ms, xs, (out, *token, block, sem) = refs[: b - a], refs[b - a : 2 * (b - a)], refs[-3 if old else -4 :]
            up = is_upper()
            for p, m_ref, x_ref in zip(parts[a:b], ms, xs):
                g = gt[p, :] + jnp.where(up, 0.0, m_ref[...].astype(F32)) + x_ref[...].astype(F32)
                block[p.start - at : p.stop - at, :] = g
            copy = pltpu.make_async_copy(block, out.at[pl.ds(at, rows), :], sem)
            copy.start()
            for ref in token:
                ref[...] = jnp.zeros(ref.shape, F32)
            copy.wait()

        ins = [gt, *back_m[a:b], *back_x[a:b]]
        return pl.pallas_call(
            k_end_texts,
            out_shape=[jax.ShapeDtypeStruct((n, d), F32), jax.ShapeDtypeStruct((8, 128), F32)][: 1 if old else 2],
            in_specs=[VMEM] * len(ins) + [HBM] * len(old) + [ANY] * len(after),
            out_specs=[HBM, VMEM][: 1 if old else 2],
            input_output_aliases={len(ins): 0} if old else {},
            scratch_shapes=[pltpu.VMEM((rows, d), F32), pltpu.SemaphoreType.DMA],
            compiler_params=pltpu.CompilerParams(vmem_limit_bytes=16 * 2**20),
            cost_estimate=pl.CostEstimate(flops=0, bytes_accessed=0, transcendentals=0),
            name=name,
        )(*ins, *old, *after)

    def k_end_images(gi, got_n, out, token):
        out[...] = gi[...] + got_n[...].astype(F32)
        token[...] = jnp.zeros(token.shape, F32)

    grad_texts, token = write_texts("end_texts_first", 0, cuts - 1, [], [])
    grad_images, token = call(
        k_end_images, "end_images", [((n, d), F32), ((8, 128), F32)], [gi_own, got_n], after=[token]
    )
    (grad_texts,) = write_texts("end_texts_last", cuts - 1, cuts, [grad_texts], [token])
    return grad_images, grad_texts


def solution(mesh):
    rows, flat = P(AXES, None), P(AXES)
    return jax.shard_map(
        local,
        mesh=mesh,
        in_specs=(rows, rows, flat, P(), P()),
        out_specs=(rows, rows),
        check_vma=False,
    )
```
